512 devices in a mesh: ex: 64 (over z, y), layer: 8 (over x, core).
Axes of the slice: x: 4, y: 4, z: 16, core: 2. Of those that a mesh axis runs over, the one named last changes fastest.
Arguments:
- query_acts: bfloat16 [8, 14336, 8192], P('layer', 'ex'), may hold values from -16 to 16
- query_grads: bfloat16 [8, 4096, 8192], P('layer', 'ex'), may hold values from -16 to 16
- proj_in: bfloat16 [8, 64, 14336], P('layer', None, 'ex'), may hold values from -0.046875 to 0.046875
- proj_out: bfloat16 [8, 64, 4096], P('layer', None, 'ex'), may hold values from -0.09375 to 0.09375
- precond_out: float32 [8, 64, 64], P('layer'), may hold values from -0.75 to 0.75
- precond_in: float32 [8, 64, 64], P('layer'), may hold values from -0.75 to 0.75
- train_sketch: bfloat16 [8, 2048, 4096], P('layer', 'ex'), may hold values from -0.5 to 0.5
Outputs:
- scores: float32 [128, 2048], P('layer', 'ex')
The draws below stay inside these ranges and needn't reach their ends.
All inputs are finite; a program needn't handle non-finite values.
Results may differ from the reference program's by a relative error of at most 0.0029.
Values may be sent and summed in bfloat16 or wider, within the bound.
A program may use at most 64 MiB of HBM per device.

```python
import jax
import jax.numpy as jnp
from jax import lax

D = 4096
FF = 14336
R = 64
QUERIES = 128
TQ = 64
LAYERS = 8
EXAMPLES = 2048


def strengthened(values, own_key, source, target, shards_of, factor):
    owner, partner = [(jnp.arange(values.shape[position]) // (values.shape[position] // shards_of)).reshape([-1 if axis == position else 1 for axis in range(values.ndim)]) for position in (source, target)]
    chosen = jax.random.permutation(own_key, shards_of)[partner]
    strong = (owner == chosen) | (owner == (partner + shards_of // 2) % shards_of)
    return jnp.where(strong, factor * values, values)


def block_levels(key, extent, shards, low, high):
    gain = 1.0
    for position, parts in shards:
        steps = jax.random.uniform(jax.random.fold_in(jax.random.fold_in(key, 6), position), (parts,), jnp.float32, low / len(shards), high / len(shards))
        gain = gain * jnp.repeat(jnp.exp(steps), extent[position] // parts).reshape((-1,) + (1,) * (len(extent) - 1 - position))
    return gain


def gaussian(own_key, dims, spread, reach, cuts=(), dtype=jnp.bfloat16):
    array = spread * jax.random.normal(own_key, dims, jnp.float32)
    if cuts:
        array = array * block_levels(own_key, dims, cuts, -0.22, 0.18)
    return jnp.clip(array, -reach, reach).astype(dtype)


def noise_with(stream_key, shape, deviation, limit, split, heavy, held_as=jnp.bfloat16):
    entries = deviation * jax.random.normal(stream_key, shape, jnp.float32)
    if split:
        entries = entries * block_levels(stream_key, shape, split, -0.22, 0.18)
    return jnp.clip(strengthened(entries, jax.random.fold_in(stream_key, 3), *heavy), -limit, limit).astype(held_as)


def setup_inputs(seed: int = 0) -> dict:
    keys = jax.random.split(jax.random.key(seed), 8)
    query_acts = noise_with(keys[0], (LAYERS, FF, QUERIES * TQ), 1.0, 16.0, ((0, 8), (1, 64)), (1, 2, 64, 4.0))
    query_grads = noise_with(keys[1], (LAYERS, D, QUERIES * TQ), 1.0, 16.0, ((0, 8), (1, 64)), (1, 2, 64, 4.0))
    proj_in = gaussian(keys[2], (LAYERS, R, FF), FF ** -0.5, 0.046875, ((0, 8), (2, 64)))
    proj_out = gaussian(keys[3], (LAYERS, R, D), D ** -0.5, 0.09375, ((0, 8), (2, 64)))
    precond_out = gaussian(keys[4], (LAYERS, R, R), R ** -0.5, 0.75, ((0, 8),), jnp.float32)
    precond_in = gaussian(keys[5], (LAYERS, R, R), R ** -0.5, 0.75, ((0, 8),), jnp.float32)
    train_sketch = gaussian(keys[6], (LAYERS, EXAMPLES, R * R), 0.08, 0.5, ((0, 8), (1, 64)))
    return dict(query_acts=query_acts, query_grads=query_grads, proj_in=proj_in, proj_out=proj_out, precond_out=precond_out, precond_in=precond_in, train_sketch=train_sketch)


def reference(query_acts, query_grads, proj_in, proj_out, precond_out, precond_in, train_sketch):
    total = jnp.zeros((QUERIES, EXAMPLES), jnp.float32)
    contract = (((0,), (1,)), ((), ()))
    for layer in range(LAYERS):
        proj_acts = lax.dot_general(query_acts[layer], proj_in[layer], contract, preferred_element_type=jnp.float32)
        proj_grads = lax.dot_general(query_grads[layer], proj_out[layer], contract, preferred_element_type=jnp.float32)
        proj_acts = proj_acts.reshape(QUERIES, TQ, R)
        proj_grads = proj_grads.reshape(QUERIES, TQ, R)
        sketch = jnp.einsum("qtr,qts->qrs", proj_grads, proj_acts, precision=lax.Precision.HIGHEST) / TQ
        left = jnp.einsum("ab,qbc->qac", precond_out[layer], sketch, precision=lax.Precision.HIGHEST)
        both = jnp.einsum("qac,cd->qad", left, precond_in[layer], precision=lax.Precision.HIGHEST)
        precond_sketch = both.astype(jnp.bfloat16).reshape(QUERIES, R * R)
        partial_value = lax.dot_general(precond_sketch, train_sketch[layer], (((1,), (1,)), ((), ())), preferred_element_type=jnp.float32)
        total = total + partial_value
    return total
```

```python
import jax
import jax.numpy as jnp
from jax import lax
from jax.sharding import PartitionSpec as P

TQ = 64


def on_device(query_acts, query_grads, proj_in, proj_out, precond_out, precond_in, train_sketch):
    rank = proj_in.shape[1]
    plain = (((1,), (0,)), ((), ()))
    last_dims = (((1,), (1,)), ((), ()))
    part_acts = lax.dot_general(proj_in[0], query_acts[0], plain, preferred_element_type=jnp.float32)
    part_grads = lax.dot_general(proj_out[0], query_grads[0], plain, preferred_element_type=jnp.float32)
    both_parts = jnp.concatenate([part_acts, part_grads], axis=0)
    summed = lax.psum_scatter(both_parts, "ex", scatter_dimension=1, tiled=True)
    own_count = summed.shape[1] // TQ
    proj_acts = summed[:rank].T.reshape(own_count, TQ, rank)
    proj_grads = summed[rank:].T.reshape(own_count, TQ, rank)
    sketch = jnp.einsum("qtr,qts->qrs", proj_grads, proj_acts, precision=lax.Precision.HIGHEST) / TQ
    left = jnp.einsum("ab,qbc->qac", precond_out[0], sketch, precision=lax.Precision.HIGHEST)
    both = jnp.einsum("qac,cd->qad", left, precond_in[0], precision=lax.Precision.HIGHEST)
    precond_sketch = both.astype(jnp.bfloat16).reshape(own_count, rank * rank)
    stored = train_sketch[0]
    partial_value = lax.dot_general(
        lax.all_gather(precond_sketch, "ex", axis=0, tiled=True),
        stored,
        last_dims,
        preferred_element_type=jnp.float32,
    )
    return lax.psum_scatter(partial_value, "layer", scatter_dimension=0, tiled=True)


def solution(mesh):
    placed = (
        P("layer", "ex", None),
        P("layer", "ex", None),
        P("layer", None, "ex"),
        P("layer", None, "ex"),
        P("layer", None, None),
        P("layer", None, None),
        P("layer", "ex", None),
    )
    return jax.shard_map(
        on_device, mesh=mesh, in_specs=placed, out_specs=P("layer", "ex"), check_vma=False
    )
```

```python
import functools

import jax
import jax.numpy as jnp
from jax import lax
from jax.experimental import pallas as pl
from jax.experimental.pallas import tpu as pltpu
from jax.sharding import PartitionSpec as P

NY = 4
R = 64
T = 128
K = 80.0
LAG1 = 2
LAG2 = 4
AGLAG = 3
MESH = pl.DeviceIdType.MESH
NT = (((1,), (1,)), ((), ()))


def encode(x):
    top = jnp.max(jnp.abs(x), axis=0, keepdims=True)
    scale = jnp.maximum(top * 1.01, 1e-36).astype(jnp.bfloat16).astype(jnp.float32)
    return jnp.exp(x * (K / scale)).astype(jnp.bfloat16), scale


def decode(code, scale):
    return jnp.log(code.astype(jnp.float32)) * (scale * (1.0 / K))


def put(ref, pieces):
    rows = 16 // len(pieces)
    scales = []
    for n, piece in enumerate(pieces):
        code, scale = encode(piece)
        ref[R * n : R * (n + 1), :] = code
        scales.append(jnp.broadcast_to(scale, (rows, T)))
    tile = scales[0] if len(scales) == 1 else jnp.concatenate(scales, axis=0)
    ref[R * len(pieces) : R * len(pieces) + 16, :] = tile.astype(jnp.bfloat16)


def get(ref, count):
    rows = 16 // count
    scales = ref[R * count : R * count + 16, :].astype(jnp.float32)
    return [
        decode(ref[R * n : R * (n + 1), :], scales[rows * n : rows * n + 1, :])
        for n in range(count)
    ]


def kernel(
    nz, nl,
    acts, grads, pin, pout, pco, pci, train, out,
    xa, xg, pa, pg, total, h1s, h1r, h2s, h2r, zs, zr, ag, xf, tr, wide, pi2, part, lr,
    sxa, sxg, str_, h1ss, h1rs, h2ss, h2rs, zss, zrs, azs, azr, y1s, y1r, y2s, y2r, lss, lrs,
):
    ne = nz * NY
    half = nz // 2
    ex = lax.axis_index("ex")
    layer = lax.axis_index("layer")
    z = ex // NY
    y = ex % NY
    up, down = (y + 1) % NY, (y + NY - 1) % NY
    across = (y + 2) % NY

    def at(zz, yy):
        return (zz * NY + yy, layer)

    y_up, y_down = at(z, up), at(z, down)

    def column(j):
        offset = jnp.where(j % 2 == 1, half - (j + 1) // 2, j // 2 - half)
        return (z + offset + nz) % nz

    def load(j):
        columns = pl.ds(pl.multiple_of(column(j) * (NY * T), NY * T), NY * T)
        return (
            pltpu.make_async_copy(acts.at[0, :, columns], xa.at[j], sxa.at[j]),
            pltpu.make_async_copy(grads.at[0, :, columns], xg.at[j], sxg.at[j]),
        )

    def start_load(j, _):
        for copy in load(j):
            copy.start()
        return 0

    lax.fori_loop(0, nz, start_load, 0)
    load_train = pltpu.make_async_copy(train.at[0], tr, str_)
    load_train.start()

    barrier = pltpu.get_barrier_semaphore()
    greeted = [y_up, y_down]
    greeted += [at((z + step + nz) % nz, y) for step in (1, -1, 2, -2)]
    greeted += [(ex, (layer + step) % nl) for step in range(1, nl)]
    for device in greeted:
        pl.semaphore_signal(barrier, inc=1, device_id=device, device_id_type=MESH)

    def remote(src, dst, ssem, rsem, device):
        return pltpu.make_async_remote_copy(
            src_ref=src, dst_ref=dst, send_sem=ssem, recv_sem=rsem,
            device_id=device, device_id_type=MESH,
        )

    def hop1(j, way):
        return remote(h1s.at[j, way], h1r.at[j, way], h1ss, h1rs.at[j, way], (y_up, y_down)[way])

    def hop2(j, way):
        return remote(h2s.at[j, way], h2r.at[j, way], h2ss, h2rs.at[j, way], (y_up, y_down)[way])

    def zstep(j):
        step = jnp.where((j == 0) | (j % 2 == 1), 1, -1)
        later = jnp.where(j == 0, 1, j + 2)
        return remote(zs.at[j], zr.at[later], zss, zrs.at[later], at((z + step + nz) % nz, y))

    def zwait(slot):
        remote(zs.at[0], zr.at[slot], zss, zrs.at[slot], at((z + 1) % nz, y)).wait_recv()

    def project(j):
        for copy in load(j):
            copy.wait()
        a = jnp.dot(pin[0], xa[j], preferred_element_type=jnp.float32)
        g = jnp.dot(pout[0], xg[j], preferred_element_type=jnp.float32)
        for d in range(NY):
            pa[j, d] = a[:, d * T : (d + 1) * T]
            pg[j, d] = g[:, d * T : (d + 1) * T]
        put(h1s.at[j, 0], [pa[j, across], pg[j, up]])
        put(h1s.at[j, 1], [pg[j, across], pa[j, down]])

        @pl.when(j == 0)
        def _():
            pl.semaphore_wait(barrier, len(greeted))

        hop1(j, 0).start()
        hop1(j, 1).start()

    def pass_on(j):
        hop1(j, 0).wait_recv()
        a_on, g_here = get(h1r.at[j, 0], 2)
        put(h2s.at[j, 0], [a_on + pa[j, up]])
        hop2(j, 0).start()
        hop1(j, 1).wait_recv()
        g_on, a_here = get(h1r.at[j, 1], 2)
        put(h2s.at[j, 1], [g_on + pg[j, down]])
        hop2(j, 1).start()
        total[j, 0] = a_here + pa[j, y]
        total[j, 1] = g_here + pg[j, y]

    def finish_y(j):
        hop2(j, 0).wait_recv()
        hop2(j, 1).wait_recv()
        (a,) = get(h2r.at[j, 0], 1)
        (g,) = get(h2r.at[j, 1], 1)
        return total[j, 0] + a, total[j, 1] + g

    def along_z(j):
        a, g = finish_y(j)
        met = (j == 1) | (j >= 3)

        @pl.when(met)
        def _():
            zwait(j)
            a_in, g_in = get(zr.at[j], 2)
            put(zs.at[j], [a + a_in, g + g_in])

        @pl.when(jnp.logical_not(met))
        def _():
            put(zs.at[j], [a, g])

        zstep(j).start()

    def turn(i, _):
        @pl.when(i < nz)
        def _():
            project(i)

        @pl.when((i >= LAG1) & (i < nz + LAG1))
        def _():
            pass_on(i - LAG1)

        @pl.when(i >= LAG2)
        def _():
            along_z(i - LAG2)

        return 0

    lax.fori_loop(0, nz - 1 + LAG2, turn, 0)

    two = jnp.concatenate([pci[0], pci[0]], axis=1)
    two = jnp.concatenate([two, two], axis=0)
    row_low = lax.broadcasted_iota(jnp.int32, (T, T), 0) < R
    lane_low = lax.broadcasted_iota(jnp.int32, (T, T), 1) < R
    pi2[...] = jnp.where(row_low == lane_low, two, 0.0)

    a, g = finish_y(nz - 1)
    for slot in (nz - 1, nz):
        zwait(slot)
        a_in, g_in = get(zr.at[slot], 2)
        a = a + a_in
        g = g + g_in
    a2 = jnp.where(row_low == lane_low, jnp.concatenate([a, a], axis=0), 0.0)
    high = lax.Precision.HIGHEST
    sketch = lax.dot_general(g, a2, NT, precision=high, preferred_element_type=jnp.float32)
    sketch = sketch * (1.0 / 64)
    left = jnp.dot(pco[0], sketch, precision=high, preferred_element_type=jnp.float32)
    both = jnp.dot(left, pi2[...], precision=high, preferred_element_type=jnp.float32)
    own = both.astype(jnp.bfloat16)
    ag[ex] = own

    def spread(e, values):
        xf[pl.ds(e, R, stride=ne), :] = values.astype(jnp.float32)

    def away(t):
        d = (t + 1) // 2
        return (z + jnp.where(t % 2 == 1, -d, d) + nz) % nz

    def gz(t, later, step):
        e = away(t) * NY + y
        return remote(ag.at[e], ag.at[e], azs, azr.at[later], at((z + step + nz) % nz, y))

    def gy1(t, way):
        e = away(t) * NY + y
        return remote(ag.at[e], ag.at[e], y1s, y1r.at[t, way], (y_up, y_down)[way])

    def gy1_wait(t, way):
        e = away(t) * NY + (down, up)[way]
        remote(ag.at[e], ag.at[e], y1s, y1r.at[t, way], (y_up, y_down)[way]).wait_recv()
        return e

    def gy2(t, way):
        e = away(t) * NY + (down, up)[way]
        rows = pl.ds(way * (R // 2), R // 2)
        return remote(
            ag.at[e, rows], ag.at[e, rows], y2s, y2r.at[t, way], (y_up, y_down)[way]
        )

    def gy2_wait(t):
        e = away(t) * NY + across
        for way in range(2):
            rows = pl.ds(way * (R // 2), R // 2)
            remote(
                ag.at[e, rows], ag.at[e, rows], y2s, y2r.at[t, way], (y_up, y_down)[way]
            ).wait_recv()
        return e

    gz(0, 1, 1).start()
    gz(0, 2, -1).start()
    gz(0, 3, 2).start()
    if nz > 4:
        gz(0, 4, -2).start()
    gy1(0, 0).start()
    gy1(0, 1).start()
    spread(ex, own)

    load_train.wait()
    lanes = lax.broadcasted_iota(jnp.int32, (tr.shape[0], T), 1) < R

    def widen(j, _):
        tile = tr[:, pl.ds(pl.multiple_of(j * T, T), T)].astype(jnp.float32)
        turned = pltpu.roll(tile, R, 1)
        first = jnp.concatenate(
            [jnp.where(lanes, tile, 0.0), jnp.where(lanes, turned, 0.0)], axis=1
        )
        second = jnp.concatenate(
            [jnp.where(lanes, 0.0, turned), jnp.where(lanes, 0.0, tile)], axis=1
        )
        full = jnp.concatenate([first, second, jnp.zeros((T - R, 2 * T), jnp.float32)], axis=0)
        wide[j] = full.astype(jnp.bfloat16)
        return 0

    lax.fori_loop(0, R // 2, widen, 0)

    remote(h1s, h1r, h1ss, h1rs.at[0, 0], y_up).wait_send()
    remote(h2s, h2r, h2ss, h2rs.at[0, 0], y_up).wait_send()
    remote(zs, zr.at[0 : nz - 1], zss, zrs.at[0], y_up).wait_send()

    def gather(t, _):
        @pl.when((t > 0) & (t < nz))
        def _():
            gz(t, t, 1).wait_recv()
            d = (t + 1) // 2
            step = jnp.where(t % 2 == 1, 1, -1)

            @pl.when((d % 2 == 0) & (t + 2 < nz))
            def _():
                gz(t, t + 2, step).start()

            @pl.when((d % 2 == 0) & (t + 4 < nz))
            def _():
                gz(t, t + 4, 2 * step).start()

            gy1(t, 0).start()
            gy1(t, 1).start()
            e = away(t) * NY + y
            spread(e, ag[e])

        @pl.when((t >= AGLAG) & (t < nz + AGLAG))
        def _():
            u = t - AGLAG
            e0 = gy1_wait(u, 0)
            gy2(u, 0).start()
            e1 = gy1_wait(u, 1)
            gy2(u, 1).start()
            spread(e0, ag[e0])
            spread(e1, ag[e1])

        @pl.when(t >= 2 * AGLAG)
        def _():
            e = gy2_wait(t - 2 * AGLAG)
            spread(e, ag[e])

        return 0

    lax.fori_loop(0, nz + 2 * AGLAG, gather, 0)

    def score(j, acc):
        x0 = xf[pl.ds(pl.multiple_of(2 * j * ne, 8), ne), :]
        x1 = xf[pl.ds(pl.multiple_of((2 * j + 1) * ne, 8), ne), :]
        x = jnp.concatenate([x0, x1], axis=1).astype(jnp.bfloat16)
        return acc + lax.dot_general(x, wide[j], NT, preferred_element_type=jnp.float32)

    part[...] = lax.fori_loop(
        0, R // 2, score, jnp.zeros((ne, T), jnp.float32), unroll=8
    )

    rows = ne // nl

    def layer_copy(step):
        target = (layer + step) % nl
        block = pl.ds(pl.multiple_of(target * rows, 8), rows)
        return remote(part.at[block], lr.at[step - 1], lss, lrs.at[step - 1], (ex, target))

    for step in range(1, nl):
        layer_copy(step).start()
    remote(ag.at[0 : nz - 1], ag.at[0 : nz - 1], azs, azr.at[0], y_up).wait_send()
    remote(ag.at[0 : 2 * nz], ag.at[0 : 2 * nz], y1s, y1r.at[0, 0], y_up).wait_send()
    remote(ag.at[0:nz], ag.at[0:nz], y2s, y2r.at[0, 0], y_up).wait_send()
    result = part[pl.ds(pl.multiple_of(layer * rows, 8), rows), :]
    for step in range(1, nl):
        layer_copy(step).wait_recv()
        result = result + lr[step - 1]
    out[...] = result
    remote(lr, lr, lss, lrs.at[0], y_up).wait_send()


def on_device(nz, nl, query_acts, query_grads, proj_in, proj_out, precond_out, precond_in, train_sketch):
    ff, d = query_acts.shape[1], query_grads.shape[1]
    examples = train_sketch.shape[1]
    ne = nz * NY
    rows = ne // nl
    bf16, f32 = jnp.bfloat16, jnp.float32
    dma = pltpu.SemaphoreType.DMA
    vmem = pl.BlockSpec(memory_space=pltpu.VMEM)
    hbm = pl.BlockSpec(memory_space=pl.ANY)
    summed = pl.pallas_call(
        functools.partial(kernel, nz, nl),
        out_shape=jax.ShapeDtypeStruct((rows, T), f32),
        in_specs=[hbm, hbm, vmem, vmem, vmem, vmem, hbm],
        out_specs=vmem,
        scratch_shapes=[
            pltpu.VMEM((nz, ff, NY * T), bf16),
            pltpu.VMEM((nz, d, NY * T), bf16),
            pltpu.VMEM((nz, NY, R, T), f32),
            pltpu.VMEM((nz, NY, R, T), f32),
            pltpu.VMEM((nz, 2, R, T), f32),
            pltpu.VMEM((nz, 2, 2 * R + 16, T), bf16),
            pltpu.VMEM((nz, 2, 2 * R + 16, T), bf16),
            pltpu.VMEM((nz, 2, R + 16, T), bf16),
            pltpu.VMEM((nz, 2, R + 16, T), bf16),
            pltpu.VMEM((nz - 1, 2 * R + 16, T), bf16),
            pltpu.VMEM((nz + 1, 2 * R + 16, T), bf16),
            pltpu.VMEM((ne, R, T), bf16),
            pltpu.VMEM((R * ne, T), f32),
            pltpu.VMEM((examples, R * R), bf16),
            pltpu.VMEM((R // 2, T, 2 * T), bf16),
            pltpu.VMEM((T, T), f32),
            pltpu.VMEM((ne, T), f32),
            pltpu.VMEM((nl - 1, rows, T), f32),
            dma((nz,)), dma((nz,)), dma,
            dma, dma((nz, 2)), dma, dma((nz, 2)),
            dma, dma((nz + 1,)),
            dma, dma((nz,)), dma, dma((nz, 2)), dma, dma((nz, 2)),
            dma, dma((nl - 1,)),
        ],
        compiler_params=pltpu.CompilerParams(
            collective_id=0, has_side_effects=True, vmem_limit_bytes=48 * 2**20
        ),
    )(query_acts, query_grads, proj_in, proj_out, precond_out, precond_in, train_sketch)
    return summed[:, : 2 * examples].reshape(2 * rows, examples)


def solution(mesh):
    nz, nl = mesh.shape["ex"] // NY, mesh.shape["layer"]
    placed = (
        P("layer", "ex", None),
        P("layer", "ex", None),
        P("layer", None, "ex"),
        P("layer", None, "ex"),
        P("layer", None, None),
        P("layer", None, None),
        P("layer", "ex", None),
    )
    return jax.shard_map(
        functools.partial(on_device, nz, nl),
        mesh=mesh, in_specs=placed, out_specs=P("layer", "ex"), check_vma=False,
    )
```

```python
import functools

import jax
import jax.numpy as jnp
from jax import lax
from jax.experimental import pallas as pl
from jax.experimental.pallas import tpu as pltpu
from jax.sharding import PartitionSpec as P

NY = 4
R = 64
T = 128
K = 80.0
LAG1 = 3
LAG2 = 6
MESH = pl.DeviceIdType.MESH
NT = (((1,), (1,)), ((), ()))


def encode(x):
    top = jnp.max(jnp.abs(x), axis=0, keepdims=True)
    scale = jnp.maximum(top * 1.01, 1e-36).astype(jnp.bfloat16).astype(jnp.float32)
    return jnp.exp(x * (K / scale)).astype(jnp.bfloat16), scale


def decode(code, scale):
    return jnp.log(code.astype(jnp.float32)) * (scale * (1.0 / K))


def put(ref, pieces):
    rows = 16 // len(pieces)
    scales = []
    for n, piece in enumerate(pieces):
        code, scale = encode(piece)
        ref[R * n : R * (n + 1), :] = code
        scales.append(jnp.broadcast_to(scale, (rows, T)))
    tile = scales[0] if len(scales) == 1 else jnp.concatenate(scales, axis=0)
    ref[R * len(pieces) : R * len(pieces) + 16, :] = tile.astype(jnp.bfloat16)


def get(ref, count):
    rows = 16 // count
    scales = ref[R * count : R * count + 16, :].astype(jnp.float32)
    return [
        decode(ref[R * n : R * (n + 1), :], scales[rows * n : rows * n + 1, :])
        for n in range(count)
    ]


def kernel(
    nz, nl,
    acts, grads, pin_in, pout_in, pco_in, pci_in, train, out,
    pin, pout, pco, pci, xa, xg, pa, pg, total, h1s, h1r, h2s, h2r, zs, zr, ag, xf, tr, wide, pi2, part, lr,
    sw, sxa, sxg, str_, h1ss, h1rs, h2ss, h2rs, zss, zrs, azs, azr, y1s, y1r, y2s, y2r, lss, lrs,
):
    ne = nz * NY
    half = nz // 2
    hub = half // 2
    ex = lax.axis_index("ex")
    layer = lax.axis_index("layer")
    z = ex // NY
    y = ex % NY
    up, down = (y + 1) % NY, (y + NY - 1) % NY
    across = (y + 2) % NY

    def at(zz, yy):
        return (zz * NY + yy, layer)

    y_up, y_down = at(z, up), at(z, down)

    def column(j):
        offset = jnp.where(j % 2 == 1, half - (j + 1) // 2, j // 2 - half)
        return (z + offset + nz) % nz

    def load(j):
        columns = pl.ds(pl.multiple_of(column(j) * (NY * T), NY * T), NY * T)
        return (
            pltpu.make_async_copy(acts.at[0, :, columns], xa.at[j], sxa.at[j]),
            pltpu.make_async_copy(grads.at[0, :, columns], xg.at[j], sxg.at[j]),
        )

    def start_load(j, _):
        for copy in load(j):
            copy.start()
        return 0

    small = [
        pltpu.make_async_copy(src, dst, sw.at[n])
        for n, (src, dst) in enumerate(
            [(pin_in, pin), (pout_in, pout), (pco_in, pco), (pci_in, pci)]
        )
    ]
    for copy in small[:2]:
        copy.start()
    lax.fori_loop(0, nz, start_load, 0)
    for copy in small[2:]:
        copy.start()
    load_train = pltpu.make_async_copy(train.at[0], tr, str_)
    load_train.start()

    barrier = pltpu.get_barrier_semaphore()
    greeted = [y_up, y_down]
    greeted += [at((z + step + nz) % nz, y) for step in (1, -1, 2, -2)]
    greeted += [(ex, (layer + step) % nl) for step in range(1, nl)]
    for device in greeted:
        pl.semaphore_signal(barrier, inc=1, device_id=device, device_id_type=MESH)

    def remote(src, dst, ssem, rsem, device):
        return pltpu.make_async_remote_copy(
            src_ref=src, dst_ref=dst, send_sem=ssem, recv_sem=rsem,
            device_id=device, device_id_type=MESH,
        )

    def hop1(j, way):
        return remote(h1s.at[j, way], h1r.at[j, way], h1ss, h1rs.at[j, way], (y_up, y_down)[way])

    def hop2(j, way):
        return remote(h2s.at[j, way], h2r.at[j, way], h2ss, h2rs.at[j, way], (y_up, y_down)[way])

    def zstep(j):
        h = (nz - j) // 2
        way = jnp.where((j == 0) | (j % 2 == 1), 1, -1)
        far = 1 - h % 2
        later = jnp.where(j == 0, 3, j + 2 + 2 * far)
        there = (z + way * (1 + far) + nz) % nz
        return remote(zs.at[j], zr.at[later, far], zss, zrs.at[later, far], at(there, y))

    def zget(slot, far):
        remote(zs.at[0], zr.at[slot, far], zss, zrs.at[slot, far], y_up).wait_recv()
        return get(zr.at[slot, far], 2)

    def project(j):
        for copy in load(j):
            copy.wait()
        a = jnp.dot(pin[0], xa[j], preferred_element_type=jnp.float32)
        g = jnp.dot(pout[0], xg[j], preferred_element_type=jnp.float32)
        for d in range(NY):
            pa[j, d] = a[:, d * T : (d + 1) * T]
            pg[j, d] = g[:, d * T : (d + 1) * T]
        put(h1s.at[j, 0], [pa[j, across], pg[j, up]])
        put(h1s.at[j, 1], [pg[j, across], pa[j, down]])

        @pl.when(j == 0)
        def _():
            pl.semaphore_wait(barrier, len(greeted))

        hop1(j, 0).start()
        hop1(j, 1).start()

    def pass_on(j):
        hop1(j, 0).wait_recv()
        a_on, g_here = get(h1r.at[j, 0], 2)
        put(h2s.at[j, 0], [a_on + pa[j, up]])
        hop2(j, 0).start()
        hop1(j, 1).wait_recv()
        g_on, a_here = get(h1r.at[j, 1], 2)
        put(h2s.at[j, 1], [g_on + pg[j, down]])
        hop2(j, 1).start()
        total[j, 0] = a_here + pa[j, y]
        total[j, 1] = g_here + pg[j, y]

    def finish_y(j):
        hop2(j, 0).wait_recv()
        hop2(j, 1).wait_recv()
        (a,) = get(h2r.at[j, 0], 1)
        (g,) = get(h2r.at[j, 1], 1)
        return total[j, 0] + a, total[j, 1] + g

    def along_z(j):
        a, g = finish_y(j)
        total[j, 0] = a
        total[j, 1] = g
        h = (nz - j) // 2

        @pl.when((h % 2 == 0) & (j > 0))
        def _():
            a_in, g_in = zget(j, 0)
            total[j, 0] += a_in
            total[j, 1] += g_in

            @pl.when((h < half - 2) | (j % 2 == 1))
            def _():
                a_in, g_in = zget(j, 1)
                total[j, 0] += a_in
                total[j, 1] += g_in

        put(zs.at[j], [total[j, 0], total[j, 1]])
        zstep(j).start()

    lanes = lax.broadcasted_iota(jnp.int32, (tr.shape[0], T), 1) < R

    def widen(j):
        tile = tr[:, pl.ds(pl.multiple_of(j * T, T), T)].astype(jnp.float32)
        turned = pltpu.roll(tile, R, 1)
        first = jnp.concatenate(
            [jnp.where(lanes, tile, 0.0), jnp.where(lanes, turned, 0.0)], axis=1
        )
        second = jnp.concatenate(
            [jnp.where(lanes, 0.0, turned), jnp.where(lanes, 0.0, tile)], axis=1
        )
        wide[j] = jnp.concatenate([first, second], axis=0).astype(jnp.bfloat16)

    def turn(i, _):
        @pl.when(i < nz)
        def _():
            project(i)

        @pl.when((i >= LAG1) & (i < nz + LAG1))
        def _():
            pass_on(i - LAG1)

        @pl.when(i >= LAG2)
        def _():
            along_z(i - LAG2)

        @pl.when(i < nz)
        def _():
            for n in range(R // 2 // nz):
                widen(i * (R // 2 // nz) + n)

        return 0

    for copy in small:
        copy.wait()
    load_train.wait()
    lax.fori_loop(0, nz - 1 + LAG2, turn, 0)

    two = jnp.concatenate([pci[0], pci[0]], axis=1)
    two = jnp.concatenate([two, two], axis=0)
    row_low = lax.broadcasted_iota(jnp.int32, (T, T), 0) < R
    lane_low = lax.broadcasted_iota(jnp.int32, (T, T), 1) < R
    pi2[...] = jnp.where(row_low == lane_low, two, 0.0)

    a, g = finish_y(nz - 1)
    for slot, far in ((nz - 1, 0), (nz, 0), (nz - 1, 1), (nz, 1)):
        a_in, g_in = zget(slot, far)
        a = a + a_in
        g = g + g_in
    a2 = jnp.where(row_low == lane_low, jnp.concatenate([a, a], axis=0), 0.0)
    high = lax.Precision.HIGHEST
    sketch = lax.dot_general(g, a2, NT, precision=high, preferred_element_type=jnp.float32)
    sketch = sketch * (1.0 / 64)
    left = jnp.dot(pco[0], sketch, precision=high, preferred_element_type=jnp.float32)
    both = jnp.dot(left, pi2[...], precision=high, preferred_element_type=jnp.float32)
    own = both.astype(jnp.bfloat16)
    ag[ex] = own

    def spread(e, values):
        xf[pl.ds(e, R, stride=ne), :] = values.astype(jnp.float32)

    def away(t):
        d = (t + 1) // 2
        return (z + jnp.where(t % 2 == 1, -d, d) + nz) % nz

    def gz(t, later, step):
        e = away(t) * NY + y
        return remote(ag.at[e], ag.at[e], azs, azr.at[later], at((z + step + nz) % nz, y))

    def gy1(t, way):
        e = away(t) * NY + y
        return remote(ag.at[e], ag.at[e], y1s, y1r.at[t, way], (y_up, y_down)[way])

    def gy1_wait(t, way):
        e = away(t) * NY + (down, up)[way]
        remote(ag.at[e], ag.at[e], y1s, y1r.at[t, way], (y_up, y_down)[way]).wait_recv()
        return e

    def gy2(t, way):
        e = away(t) * NY + (down, up)[way]
        rows = pl.ds(way * (R // 2), R // 2)
        return remote(
            ag.at[e, rows], ag.at[e, rows], y2s, y2r.at[t, way], (y_up, y_down)[way]
        )

    def gy2_wait(t):
        e = away(t) * NY + across
        for way in range(2):
            rows = pl.ds(way * (R // 2), R // 2)
            remote(
                ag.at[e, rows], ag.at[e, rows], y2s, y2r.at[t, way], (y_up, y_down)[way]
            ).wait_recv()
        return e

    for d in [hub, hub + 1] + list(range(hub - 1, 0, -1)):
        gz(0, 2 * d - 1, d).start()
        gz(0, 2 * d, -d).start()
    gy1(0, 0).start()
    gy1(0, 1).start()


    remote(h1s, h1r, h1ss, h1rs.at[0, 0], y_up).wait_send()
    remote(h2s, h2r, h2ss, h2rs.at[0, 0], y_up).wait_send()
    remote(zs, zr.at[0 : nz - 1, 0], zss, zrs.at[0, 0], y_up).wait_send()

    first = 2 * (hub + 1) + 1

    def chunk(n):
        pair, side = (n - 1) // 2, (n - 1) % 2
        early = 2 * jnp.where(pair < hub, hub - pair, hub + 1) - 1 + side
        m = n - first - 1
        late = jnp.where(n == first, nz - 1, nz - 3 - 2 * (m // 2) + (m + 2) % 2)
        return jnp.where(n == 0, 0, jnp.where(n < first, early, late))

    def arrived(t):
        gz(t, t, 1).wait_recv()

    arrived(2 * hub - 1)
    for d in range(half, hub + 1, -1):
        gz(2 * hub - 1, 2 * d - 1, d - hub).start()
    arrived(2 * hub)
    for d in range(half - 1, hub + 1, -1):
        gz(2 * hub, 2 * d, hub - d).start()

    def forward(n, _):
        t = chunk(n)

        @pl.when(n > 2)
        def _():
            arrived(t)

        gy1(t, 0).start()
        gy1(t, 1).start()
        return 0

    def forward_half(n, _):
        t = chunk(n)
        gy1_wait(t, 0)
        gy2(t, 0).start()
        gy1_wait(t, 1)
        gy2(t, 1).start()
        return 0

    def gy3(t, yy):
        e = away(t) * NY + yy
        return remote(ag.at[e], ag.at[e], y2s, y2r.at[t, 0], at(z, across))

    def forward_late(n, _):
        t = chunk(n)
        arrived(t)
        gy3(t, y).start()
        gy1(t, 0).start()
        gy1(t, 1).start()
        return 0

    def spread_three(n, _):
        t = chunk(n)
        for yy in (y, down, up):
            e = away(t) * NY + yy
            spread(e, ag[e])
        return 0

    def spread_last(n, _):
        e = gy2_wait(chunk(n))
        spread(e, ag[e])
        return 0

    def spread_late(n, _):
        t = chunk(n)
        e = away(t) * NY + y
        spread(e, ag[e])
        for way in range(2):
            e = gy1_wait(t, way)
            spread(e, ag[e])
        gy3(t, across).wait_recv()
        e = away(t) * NY + across
        spread(e, ag[e])
        return 0

    lax.fori_loop(1, first, forward, 0)
    lax.fori_loop(0, first, forward_half, 0)
    lax.fori_loop(first, nz, forward_late, 0)
    lax.fori_loop(0, first, spread_three, 0)
    lax.fori_loop(0, first, spread_last, 0)
    lax.fori_loop(first, nz, spread_late, 0)

    def score(j, acc):
        x0 = xf[pl.ds(pl.multiple_of(2 * j * ne, 8), ne), :]
        x1 = xf[pl.ds(pl.multiple_of((2 * j + 1) * ne, 8), ne), :]
        x = jnp.concatenate([x0, x1], axis=1).astype(jnp.bfloat16)
        return acc + lax.dot_general(x, wide[j], NT, preferred_element_type=jnp.float32)

    count = wide.shape[1]
    scores = lax.fori_loop(0, R // 2, score, jnp.zeros((ne, count), jnp.float32), unroll=8)
    part[...] = jnp.concatenate([scores, jnp.zeros((ne, T - count), jnp.float32)], axis=1)

    rows = ne // nl

    def layer_copy(step):
        target = (layer + step) % nl
        block = pl.ds(pl.multiple_of(target * rows, 8), rows)
        return remote(part.at[block], lr.at[step - 1], lss, lrs.at[step - 1], (ex, target))

    for step in range(1, nl):
        layer_copy(step).start()
    remote(ag.at[0 : nz - 1], ag.at[0 : nz - 1], azs, azr.at[0], y_up).wait_send()
    remote(ag.at[0 : 2 * nz], ag.at[0 : 2 * nz], y1s, y1r.at[0, 0], y_up).wait_send()
    remote(ag.at[0:nz], ag.at[0:nz], y2s, y2r.at[0, 0], y_up).wait_send()
    result = part[pl.ds(pl.multiple_of(layer * rows, 8), rows), :]
    for step in range(1, nl):
        layer_copy(step).wait_recv()
        result = result + lr[step - 1]
    out[...] = result
    remote(lr, lr, lss, lrs.at[0], y_up).wait_send()


def on_device(nz, nl, query_acts, query_grads, proj_in, proj_out, precond_out, precond_in, train_sketch):
    ff, d = query_acts.shape[1], query_grads.shape[1]
    examples = train_sketch.shape[1]
    ne = nz * NY
    rows = ne // nl
    bf16, f32 = jnp.bfloat16, jnp.float32
    dma = pltpu.SemaphoreType.DMA
    vmem = pl.BlockSpec(memory_space=pltpu.VMEM)
    hbm = pl.BlockSpec(memory_space=pl.ANY)
    summed = pl.pallas_call(
        functools.partial(kernel, nz, nl),
        out_shape=jax.ShapeDtypeStruct((rows, T), f32),
        in_specs=[hbm] * 7,
        out_specs=vmem,
        scratch_shapes=[
            pltpu.VMEM(proj_in.shape, bf16),
            pltpu.VMEM(proj_out.shape, bf16),
            pltpu.VMEM(precond_out.shape, f32),
            pltpu.VMEM(precond_in.shape, f32),
            pltpu.VMEM((nz, ff, NY * T), bf16),
            pltpu.VMEM((nz, d, NY * T), bf16),
            pltpu.VMEM((nz, NY, R, T), f32),
            pltpu.VMEM((nz, NY, R, T), f32),
            pltpu.VMEM((nz, 2, R, T), f32),
            pltpu.VMEM((nz, 2, 2 * R + 16, T), bf16),
            pltpu.VMEM((nz, 2, 2 * R + 16, T), bf16),
            pltpu.VMEM((nz, 2, R + 16, T), bf16),
            pltpu.VMEM((nz, 2, R + 16, T), bf16),
            pltpu.VMEM((nz - 1, 2 * R + 16, T), bf16),
            pltpu.VMEM((nz + 1, 2, 2 * R + 16, T), bf16),
            pltpu.VMEM((ne, R, T), bf16),
            pltpu.VMEM((R * ne, T), f32),
            pltpu.VMEM((examples, R * R), bf16),
            pltpu.VMEM((R // 2, 2 * examples, 2 * T), bf16),
            pltpu.VMEM((T, T), f32),
            pltpu.VMEM((ne, T), f32),
            pltpu.VMEM((nl - 1, rows, T), f32),
            dma((4,)), dma((nz,)), dma((nz,)), dma,
            dma, dma((nz, 2)), dma, dma((nz, 2)),
            dma, dma((nz + 1, 2)),
            dma, dma((nz,)), dma, dma((nz, 2)), dma, dma((nz, 2)),
            dma, dma((nl - 1,)),
        ],
        compiler_params=pltpu.CompilerParams(
            collective_id=0, has_side_effects=True, vmem_limit_bytes=60 * 2**20
        ),
    )(query_acts, query_grads, proj_in, proj_out, precond_out, precond_in, train_sketch)
    return summed[:, : 2 * examples].reshape(2 * rows, examples)


def solution(mesh):
    nz, nl = mesh.shape["ex"] // NY, mesh.shape["layer"]
    placed = (
        P("layer", "ex", None),
        P("layer", "ex", None),
        P("layer", None, "ex"),
        P("layer", None, "ex"),
        P("layer", None, None),
        P("layer", None, None),
        P("layer", "ex", None),
    )
    return jax.shard_map(
        functools.partial(on_device, nz, nl),
        mesh=mesh, in_specs=placed, out_specs=P("layer", "ex"), check_vma=False,
    )
```

```python
import functools

import jax
import jax.numpy as jnp
from jax import lax
from jax.experimental import pallas as pl
from jax.experimental.pallas import tpu as pltpu
from jax.sharding import PartitionSpec as P

NY = 4
R = 64
T = 128
K = 80.0
LAG1 = 3
WIDEN = 4
LAG2 = 6
ND = 1
MESH = pl.DeviceIdType.MESH
NT = (((1,), (1,)), ((), ()))


def encode(x):
    top = jnp.max(jnp.abs(x), axis=0, keepdims=True)
    scale = jnp.maximum(top * 1.01, 1e-36).astype(jnp.bfloat16).astype(jnp.float32)
    return jnp.exp(x * (K / scale)).astype(jnp.bfloat16), scale


def decode(code, scale):
    return jnp.log(code.astype(jnp.float32)) * (scale * (1.0 / K))


def put(ref, pieces):
    row = lax.broadcasted_iota(jnp.int32, (16, T), 0)
    span = 16 // len(pieces)
    tile = jnp.zeros((16, T), jnp.float32)
    for n, piece in enumerate(pieces):
        code, scale = encode(piece)
        ref[R * n : R * (n + 1), :] = code
        tile = jnp.where(row < span * n, tile, scale)
    ref[R * len(pieces) : R * len(pieces) + 16, :] = tile.astype(jnp.bfloat16)


def get(ref, count):
    span = 16 // count
    scales = ref[R * count : R * count + 16, :].astype(jnp.float32)
    return [
        decode(ref[R * n : R * (n + 1), :], scales[span * n : span * n + 1, :])
        for n in range(count)
    ]


def kernel(
    nz, nl,
    acts, grads, pin_in, pout_in, pco_in, pci_in, train, out,
    pin, pout, pco, pci, xa, xg, pa, pg, total, h1s, h1r, h2s, h2r, ds, dr, fs, fr, zs, zr, ag, xf, tr, wide, pi2, part, lr,
    sw, sxa, sxg, str_, h1ss, h1rs, h2ss, h2rs, dss, drs, fss, frs, zss, zrs, azs, azr, y1s, y1r, y2s, y2r, lss, lrs,
):
    ne = nz * NY
    half = nz // 2
    hub = half // 2
    ex = lax.axis_index("ex")
    layer = lax.axis_index("layer")
    z = ex // NY
    y = ex % NY
    up, down = (y + 1) % NY, (y + NY - 1) % NY
    across = (y + 2) % NY

    def at(zz, yy):
        return (zz * NY + yy, layer)

    y_up, y_down = at(z, up), at(z, down)

    def column(j):
        offset = jnp.where(j % 2 == 1, half - (j + 1) // 2, j // 2 - half)
        return (z + offset + nz) % nz

    def load(j):
        columns = pl.ds(pl.multiple_of(column(j) * (NY * T), NY * T), NY * T)
        return (
            pltpu.make_async_copy(acts.at[0, :, columns], xa.at[j], sxa.at[j]),
            pltpu.make_async_copy(grads.at[0, :, columns], xg.at[j], sxg.at[j]),
        )

    def start_load(j, _):
        for copy in load(j):
            copy.start()
        return 0

    small = [
        pltpu.make_async_copy(src, dst, sw.at[n])
        for n, (src, dst) in enumerate(
            [(pin_in, pin), (pout_in, pout), (pco_in, pco), (pci_in, pci)]
        )
    ]
    for copy in small[:2]:
        copy.start()
    lax.fori_loop(0, nz, start_load, 0)
    for copy in small[2:]:
        copy.start()
    load_train = pltpu.make_async_copy(train.at[0], tr, str_)
    load_train.start()

    barrier = pltpu.get_barrier_semaphore()
    greeted = [y_up, y_down, at(z, across)]
    greeted += [at((z + step + nz) % nz, y) for step in (1, -1, 2, -2)]
    greeted += [(ex, (layer + step) % nl) for step in range(1, nl)]
    for device in greeted:
        pl.semaphore_signal(barrier, inc=1, device_id=device, device_id_type=MESH)

    def remote(src, dst, ssem, rsem, device):
        return pltpu.make_async_remote_copy(
            src_ref=src, dst_ref=dst, send_sem=ssem, recv_sem=rsem,
            device_id=device, device_id_type=MESH,
        )

    def hop1(j, way):
        return remote(h1s.at[j, way], h1r.at[j, way], h1ss, h1rs.at[j, way], (y_up, y_down)[way])

    def hop2(j, way):
        return remote(h2s.at[j, way], h2r.at[j, way], h2ss, h2rs.at[j, way], (y_up, y_down)[way])

    def zstep(j):
        h = (nz - j) // 2
        way = jnp.where((j == 0) | (j % 2 == 1), 1, -1)
        far = 1 - h % 2
        later = jnp.where(j == 0, 3, j + 2 + 2 * far)
        there = (z + way * (1 + far) + nz) % nz
        return remote(zs.at[j], zr.at[later, far], zss, zrs.at[later, far], at(there, y))

    last = nz - 3

    def straight(j):
        target = at(z, across)
        n = j - (last + 1 - ND)
        return remote(ds.at[n], dr.at[n], dss, drs.at[n], target)

    def neighbour(side):
        there = at((z + (1, -1)[side] + nz) % nz, y)
        return remote(fs.at[side], fr.at[side], fss, frs.at[side], there)

    def zget(slot, far):
        remote(zs.at[0], zr.at[slot, far], zss, zrs.at[slot, far], y_up).wait_recv()
        return get(zr.at[slot, far], 2)

    def project(j, place):
        for copy in load(place):
            copy.wait()
        a = jnp.dot(pin[0], xa[place], preferred_element_type=jnp.float32)
        g = jnp.dot(pout[0], xg[place], preferred_element_type=jnp.float32)
        for d in range(NY):
            pa[j, d] = a[:, d * T : (d + 1) * T]
            pg[j, d] = g[:, d * T : (d + 1) * T]

    def first_hop(j):
        put(h1s.at[j, 0], [pa[j, across], pg[j, up]])
        put(h1s.at[j, 1], [pg[j, across], pa[j, down]])

    def send_first_hop(j):
        hop1(j, 0).start()
        hop1(j, 1).start()

    def send_straight(j):
        put(ds.at[j - (last + 1 - ND)], [pa[j, across], pg[j, across]])
        straight(j).start()
        put(h1s.at[j, 0], [pa[j, up], pg[j, up]])
        hop1(j, 0).start()
        put(h1s.at[j, 1], [pa[j, down], pg[j, down]])
        hop1(j, 1).start()

    def to_neighbour(side):
        place = nz - 3 + side
        project(place, place)
        put(fs.at[side], [p[place, d] for d in range(NY) for p in (pa, pg)])

    def from_neighbour(side):
        neighbour(side).wait_recv()
        pieces = get(fr.at[side], 2 * NY)
        for d in range(NY):
            pa[last, d] += pieces[2 * d]
            pg[last, d] += pieces[2 * d + 1]

    def pass_on(j):
        hop1(j, 0).wait_recv()
        a_on, g_here = get(h1r.at[j, 0], 2)
        put(h2s.at[j, 0], [a_on + pa[j, up]])
        hop2(j, 0).start()
        hop1(j, 1).wait_recv()
        g_on, a_here = get(h1r.at[j, 1], 2)
        put(h2s.at[j, 1], [g_on + pg[j, down]])
        hop2(j, 1).start()
        total[j, 0] = a_here + pa[j, y]
        total[j, 1] = g_here + pg[j, y]

    def finish_y(j):
        hop2(j, 0).wait_recv()
        hop2(j, 1).wait_recv()
        (a,) = get(h2r.at[j, 0], 1)
        (g,) = get(h2r.at[j, 1], 1)
        total[j, 0] += a
        total[j, 1] += g

    def finish_straight(j):
        hop1(j, 0).wait_recv()
        a0, g0 = get(h1r.at[j, 0], 2)
        hop1(j, 1).wait_recv()
        a1, g1 = get(h1r.at[j, 1], 2)
        straight(j).wait_recv()
        a2, g2 = get(dr.at[j - (last + 1 - ND)], 2)
        total[j, 0] = a0 + a1 + a2 + pa[j, y]
        total[j, 1] = g0 + g1 + g2 + pg[j, y]

    def along_z(j):
        @pl.when(j <= last - ND)
        def _():
            finish_y(j)

        @pl.when(j > last - ND)
        def _():
            finish_straight(j)

        h = (nz - j) // 2

        @pl.when((h % 2 == 0) & (j > 0))
        def _():
            a_in, g_in = zget(j, 0)
            total[j, 0] += a_in
            total[j, 1] += g_in

            @pl.when((h < half - 2) | (j % 2 == 1))
            def _():
                a_in, g_in = zget(j, 1)
                total[j, 0] += a_in
                total[j, 1] += g_in

        put(zs.at[j], [total[j, 0], total[j, 1]])
        zstep(j).start()

    lanes = lax.broadcasted_iota(jnp.int32, (tr.shape[0], T), 1) < R

    def widen(j):
        tile = tr[:, pl.ds(pl.multiple_of(j * T, T), T)].astype(jnp.float32)
        turned = pltpu.roll(tile, R, 1)
        first = jnp.concatenate(
            [jnp.where(lanes, tile, 0.0), jnp.where(lanes, turned, 0.0)], axis=1
        )
        second = jnp.concatenate(
            [jnp.where(lanes, 0.0, turned), jnp.where(lanes, 0.0, tile)], axis=1
        )
        wide[j] = jnp.concatenate([first, second], axis=0).astype(jnp.bfloat16)

    def turn(i, _):
        @pl.when((i > 0) & (i < last))
        def _():
            project(i, i)

        @pl.when((i > 0) & (i <= last - ND))
        def _():
            first_hop(i)
            send_first_hop(i)

        @pl.when((i > last - ND) & (i < last))
        def _():
            send_straight(i)

        @pl.when(i == last)
        def _():
            project(last, nz - 1)
            from_neighbour(0)
            from_neighbour(1)
            send_straight(last)

        @pl.when((i >= LAG1) & (i <= last - ND + LAG1))
        def _():
            pass_on(i - LAG1)

        @pl.when(i >= LAG2)
        def _():
            along_z(i - LAG2)

        @pl.when(i < WIDEN)
        def _():
            for n in range(R // 2 // WIDEN):
                widen(i * (R // 2 // WIDEN) + n)

        return 0

    for copy in small:
        copy.wait()
    project(0, 0)
    first_hop(0)
    to_neighbour(0)
    to_neighbour(1)
    pl.semaphore_wait(barrier, len(greeted))
    send_first_hop(0)
    neighbour(0).start()
    neighbour(1).start()
    load_train.wait()
    lax.fori_loop(0, last + LAG2, turn, 0)

    two = jnp.concatenate([pci[0], pci[0]], axis=1)
    two = jnp.concatenate([two, two], axis=0)
    row_low = lax.broadcasted_iota(jnp.int32, (T, T), 0) < R
    lane_low = lax.broadcasted_iota(jnp.int32, (T, T), 1) < R
    pi2[...] = jnp.where(row_low == lane_low, two, 0.0)

    finish_straight(last)
    a, g = total[last, 0], total[last, 1]
    for slot in (nz - 1, nz):
        a_in, g_in = zget(slot, 1)
        a = a + a_in
        g = g + g_in
    a2 = jnp.where(row_low == lane_low, jnp.concatenate([a, a], axis=0), 0.0)
    high = lax.Precision.HIGHEST
    sketch = lax.dot_general(g, a2, NT, precision=high, preferred_element_type=jnp.float32)
    sketch = sketch * (1.0 / 64)
    left = jnp.dot(pco[0], sketch, precision=high, preferred_element_type=jnp.float32)
    both = jnp.dot(left, pi2[...], precision=high, preferred_element_type=jnp.float32)
    own = both.astype(jnp.bfloat16)
    ag[ex] = own

    def spread(e, values):
        xf[pl.ds(e, R, stride=ne), :] = values.astype(jnp.float32)

    def away(t):
        d = (t + 1) // 2
        return (z + jnp.where(t % 2 == 1, -d, d) + nz) % nz

    def gz(t, later, step):
        e = away(t) * NY + y
        return remote(ag.at[e], ag.at[e], azs, azr.at[later], at((z + step + nz) % nz, y))

    def gy1(t, way):
        e = away(t) * NY + y
        return remote(ag.at[e], ag.at[e], y1s, y1r.at[t, way], (y_up, y_down)[way])

    def gy1_wait(t, way):
        e = away(t) * NY + (down, up)[way]
        remote(ag.at[e], ag.at[e], y1s, y1r.at[t, way], (y_up, y_down)[way]).wait_recv()
        return e

    def gy2(t, way):
        e = away(t) * NY + (down, up)[way]
        rows = pl.ds(way * (R // 2), R // 2)
        return remote(
            ag.at[e, rows], ag.at[e, rows], y2s, y2r.at[t, way], (y_up, y_down)[way]
        )

    def gy2_wait(t):
        e = away(t) * NY + across
        for way in range(2):
            rows = pl.ds(way * (R // 2), R // 2)
            remote(
                ag.at[e, rows], ag.at[e, rows], y2s, y2r.at[t, way], (y_up, y_down)[way]
            ).wait_recv()
        return e

    for d in [hub, hub + 1] + list(range(hub - 1, 0, -1)):
        gz(0, 2 * d - 1, d).start()
        gz(0, 2 * d, -d).start()
    gy1(0, 0).start()
    gy1(0, 1).start()


    for sent, sem in ((h1s, h1ss), (h2s, h2ss), (ds, dss), (fs, fss), (zs, zss)):
        remote(sent, sent, sem, azr.at[0], y_up).wait_send()

    first = 2 * (hub + 1) + 1

    def chunk(n):
        pair, side = (n - 1) // 2, (n - 1) % 2
        early = 2 * jnp.where(pair < hub, hub - pair, hub + 1) - 1 + side
        m = n - first - 1
        late = jnp.where(n == first, nz - 1, nz - 3 - 2 * (m // 2) + (m + 2) % 2)
        return jnp.where(n == 0, 0, jnp.where(n < first, early, late))

    def arrived(t):
        gz(t, t, 1).wait_recv()

    arrived(2 * hub - 1)
    for d in range(half, hub + 1, -1):
        gz(2 * hub - 1, 2 * d - 1, d - hub).start()
    arrived(2 * hub)
    for d in range(half - 1, hub + 1, -1):
        gz(2 * hub, 2 * d, hub - d).start()

    def forward(n, _):
        t = chunk(n)

        @pl.when(n > 2)
        def _():
            arrived(t)

        gy1(t, 0).start()
        gy1(t, 1).start()
        return 0

    def forward_half(n, _):
        t = chunk(n)
        gy1_wait(t, 0)
        gy2(t, 0).start()
        gy1_wait(t, 1)
        gy2(t, 1).start()
        return 0

    def gy3(t, yy):
        e = away(t) * NY + yy
        return remote(ag.at[e], ag.at[e], y2s, y2r.at[t, 0], at(z, across))

    def forward_late(n, _):
        t = chunk(n)
        arrived(t)
        gy3(t, y).start()
        gy1(t, 0).start()
        gy1(t, 1).start()
        return 0

    def spread_three(n, _):
        t = chunk(n)
        for yy in (y, down, up):
            e = away(t) * NY + yy
            spread(e, ag[e])
        return 0

    def spread_last(n, _):
        e = gy2_wait(chunk(n))
        spread(e, ag[e])
        return 0

    def spread_late(n, _):
        t = chunk(n)
        e = away(t) * NY + y
        spread(e, ag[e])
        for way in range(2):
            e = gy1_wait(t, way)
            spread(e, ag[e])
        gy3(t, across).wait_recv()
        e = away(t) * NY + across
        spread(e, ag[e])
        return 0

    lax.fori_loop(1, first, forward, 0)
    lax.fori_loop(0, first, forward_half, 0)
    lax.fori_loop(first, nz, forward_late, 0)
    lax.fori_loop(0, first, spread_three, 0)
    lax.fori_loop(0, first, spread_last, 0)
    lax.fori_loop(first, nz, spread_late, 0)

    def score(j, acc):
        x0 = xf[pl.ds(pl.multiple_of(2 * j * ne, 8), ne), :]
        x1 = xf[pl.ds(pl.multiple_of((2 * j + 1) * ne, 8), ne), :]
        x = jnp.concatenate([x0, x1], axis=1).astype(jnp.bfloat16)
        return acc + lax.dot_general(x, wide[j], NT, preferred_element_type=jnp.float32)

    count = wide.shape[1]
    scores = lax.fori_loop(0, R // 2, score, jnp.zeros((ne, count), jnp.float32), unroll=8)
    part[...] = jnp.concatenate([scores, jnp.zeros((ne, T - count), jnp.float32)], axis=1)

    rows = ne // nl

    def layer_copy(step):
        target = (layer + step) % nl
        block = pl.ds(pl.multiple_of(target * rows, 8), rows)
        return remote(part.at[block], lr.at[step - 1], lss, lrs.at[step - 1], (ex, target))

    for step in range(1, nl):
        layer_copy(step).start()
    remote(ag.at[0 : nz - 1], ag.at[0 : nz - 1], azs, azr.at[0], y_up).wait_send()
    remote(ag.at[0 : 2 * nz], ag.at[0 : 2 * nz], y1s, y1r.at[0, 0], y_up).wait_send()
    remote(ag.at[0:nz], ag.at[0:nz], y2s, y2r.at[0, 0], y_up).wait_send()
    result = part[pl.ds(pl.multiple_of(layer * rows, 8), rows), :]
    for step in range(1, nl):
        layer_copy(step).wait_recv()
        result = result + lr[step - 1]
    out[...] = result
    remote(lr, lr, lss, lrs.at[0], y_up).wait_send()


def on_device(nz, nl, query_acts, query_grads, proj_in, proj_out, precond_out, precond_in, train_sketch):
    ff, d = query_acts.shape[1], query_grads.shape[1]
    examples = train_sketch.shape[1]
    ne = nz * NY
    rows = ne // nl
    bf16, f32 = jnp.bfloat16, jnp.float32
    dma = pltpu.SemaphoreType.DMA
    vmem = pl.BlockSpec(memory_space=pltpu.VMEM)
    hbm = pl.BlockSpec(memory_space=pl.ANY)
    summed = pl.pallas_call(
        functools.partial(kernel, nz, nl),
        out_shape=jax.ShapeDtypeStruct((rows, T), f32),
        in_specs=[hbm] * 7,
        out_specs=vmem,
        scratch_shapes=[
            pltpu.VMEM(proj_in.shape, bf16),
            pltpu.VMEM(proj_out.shape, bf16),
            pltpu.VMEM(precond_out.shape, f32),
            pltpu.VMEM(precond_in.shape, f32),
            pltpu.VMEM((nz, ff, NY * T), bf16),
            pltpu.VMEM((nz, d, NY * T), bf16),
            pltpu.VMEM((nz, NY, R, T), f32),
            pltpu.VMEM((nz, NY, R, T), f32),
            pltpu.VMEM((nz, 2, R, T), f32),
            pltpu.VMEM((nz - 2, 2, 2 * R + 16, T), bf16),
            pltpu.VMEM((nz - 2, 2, 2 * R + 16, T), bf16),
            pltpu.VMEM((nz - 2 - ND, 2, R + 16, T), bf16),
            pltpu.VMEM((nz - 2 - ND, 2, R + 16, T), bf16),
            pltpu.VMEM((ND, 2 * R + 16, T), bf16),
            pltpu.VMEM((ND, 2 * R + 16, T), bf16),
            pltpu.VMEM((2, 2 * NY * R + 16, T), bf16),
            pltpu.VMEM((2, 2 * NY * R + 16, T), bf16),
            pltpu.VMEM((nz - 3, 2 * R + 16, T), bf16),
            pltpu.VMEM((nz + 1, 2, 2 * R + 16, T), bf16),
            pltpu.VMEM((ne, R, T), bf16),
            pltpu.VMEM((R * ne, T), f32),
            pltpu.VMEM((examples, R * R), bf16),
            pltpu.VMEM((R // 2, 2 * examples, 2 * T), bf16),
            pltpu.VMEM((T, T), f32),
            pltpu.VMEM((ne, T), f32),
            pltpu.VMEM((nl - 1, rows, T), f32),
            dma((4,)), dma((nz,)), dma((nz,)), dma,
            dma, dma((nz, 2)), dma, dma((nz, 2)), dma, dma((ND,)), dma, dma((2,)),
            dma, dma((nz + 1, 2)),
            dma, dma((nz,)), dma, dma((nz, 2)), dma, dma((nz, 2)),
            dma, dma((nl - 1,)),
        ],
        compiler_params=pltpu.CompilerParams(
            collective_id=0, has_side_effects=True, vmem_limit_bytes=60 * 2**20
        ),
    )(query_acts, query_grads, proj_in, proj_out, precond_out, precond_in, train_sketch)
    return summed[:, : 2 * examples].reshape(2 * rows, examples)


def solution(mesh):
    nz, nl = mesh.shape["ex"] // NY, mesh.shape["layer"]
    placed = (
        P("layer", "ex", None),
        P("layer", "ex", None),
        P("layer", None, "ex"),
        P("layer", None, "ex"),
        P("layer", None, None),
        P("layer", None, None),
        P("layer", "ex", None),
    )
    return jax.shard_map(
        functools.partial(on_device, nz, nl),
        mesh=mesh, in_specs=placed, out_specs=P("layer", "ex"), check_vma=False,
    )
```

```python
import functools

import jax
import jax.numpy as jnp
from jax import lax
from jax.experimental import pallas as pl
from jax.experimental.pallas import tpu as pltpu
from jax.sharding import PartitionSpec as P

NY = 4
R = 64
T = 128
K = 80.0
LAG1 = 3
WIDEN = 4
LAG2 = 6
ND = 1
XD = 1
MESH = pl.DeviceIdType.MESH
NT = (((1,), (1,)), ((), ()))


def encode(x):
    top = jnp.max(jnp.abs(x), axis=0, keepdims=True)
    scale = jnp.maximum(top * 1.01, 1e-36).astype(jnp.bfloat16).astype(jnp.float32)
    return jnp.exp(x * (K / scale)).astype(jnp.bfloat16), scale


def decode(code, scale):
    return jnp.log(code.astype(jnp.float32)) * (scale * (1.0 / K))


def put(ref, pieces):
    row = lax.broadcasted_iota(jnp.int32, (16, T), 0)
    span = 16 // len(pieces)
    tile = jnp.zeros((16, T), jnp.float32)
    for n, piece in enumerate(pieces):
        code, scale = encode(piece)
        ref[R * n : R * (n + 1), :] = code
        tile = jnp.where(row < span * n, tile, scale)
    ref[R * len(pieces) : R * len(pieces) + 16, :] = tile.astype(jnp.bfloat16)


def get(ref, count):
    span = 16 // count
    scales = ref[R * count : R * count + 16, :].astype(jnp.float32)
    return [
        decode(ref[R * n : R * (n + 1), :], scales[span * n : span * n + 1, :])
        for n in range(count)
    ]


def kernel(
    nz, nl,
    acts, grads, pin_in, pout_in, pco_in, pci_in, train, out,
    pin, pout, pco, pci, xa, xg, pa, pg, total, h1s, h1r, h2s, h2r, ds, dr, fs, fr, zs, zr, ag, xf, tr, wide, pi2, part, lr,
    sw, sxa, sxg, str_, h1ss, h1rs, h2ss, h2rs, dss, drs, fss, frs, zss, zrs, told_1, told_2, azs, azr, y1s, y1r, y2s, y2r, lss, lrs,
):
    ne = nz * NY
    half = nz // 2
    hub = half // 2
    ex = lax.axis_index("ex")
    layer = lax.axis_index("layer")
    z = ex // NY
    y = ex % NY
    up, down = (y + 1) % NY, (y + NY - 1) % NY
    across = (y + 2) % NY

    def at(zz, yy):
        return (zz * NY + yy, layer)

    y_up, y_down = at(z, up), at(z, down)

    def column(j):
        offset = jnp.where(j % 2 == 1, half - (j + 1) // 2, j // 2 - half)
        return (z + offset + nz) % nz

    def load(j):
        columns = pl.ds(pl.multiple_of(column(j) * (NY * T), NY * T), NY * T)
        return (
            pltpu.make_async_copy(acts.at[0, :, columns], xa.at[j], sxa.at[j]),
            pltpu.make_async_copy(grads.at[0, :, columns], xg.at[j], sxg.at[j]),
        )

    def start_load(j, _):
        for copy in load(j):
            copy.start()
        return 0

    small = [
        pltpu.make_async_copy(src, dst, sw.at[n])
        for n, (src, dst) in enumerate(
            [(pin_in, pin), (pout_in, pout), (pco_in, pco), (pci_in, pci)]
        )
    ]
    for copy in small[:2]:
        copy.start()
    lax.fori_loop(0, nz, start_load, 0)
    for copy in small[2:]:
        copy.start()
    load_train = pltpu.make_async_copy(train.at[0], tr, str_)
    load_train.start()

    barrier = pltpu.get_barrier_semaphore()
    z_near = [at((z + step + nz) % nz, y) for step in (1, -1)]
    if nl == 8:
        x_near = [(ex, (layer + step) % nl) for step in (2, nl - 2)]
        greeted = [y_up, y_down] + z_near + x_near + [(ex, layer + 1 - 2 * (layer % 2))]
        tell_1, tell_2 = greeted[2:], x_near
    else:
        greeted = [y_up, y_down] + z_near + [(ex, (layer + step) % nl) for step in range(1, nl)]
        tell_1, tell_2 = z_near, z_near

    def tell(devices, sem):
        for device in devices:
            pl.semaphore_signal(sem, inc=1, device_id=device, device_id_type=MESH)

    for device in greeted:
        pl.semaphore_signal(barrier, inc=1, device_id=device, device_id_type=MESH)

    def remote(src, dst, ssem, rsem, device):
        return pltpu.make_async_remote_copy(
            src_ref=src, dst_ref=dst, send_sem=ssem, recv_sem=rsem,
            device_id=device, device_id_type=MESH,
        )

    def hop1(j, way):
        return remote(h1s.at[j, way], h1r.at[j, way], h1ss, h1rs.at[j, way], (y_up, y_down)[way])

    def hop2(j, way):
        return remote(h2s.at[j, way], h2r.at[j, way], h2ss, h2rs.at[j, way], (y_up, y_down)[way])

    def zstep(j):
        h = (nz - j) // 2
        way = jnp.where((j == 0) | (j % 2 == 1), 1, -1)
        far = 1 - h % 2
        later = jnp.where(j == 0, 3, j + 2 + 2 * far)
        there = (z + way * (1 + far) + nz) % nz
        return remote(zs.at[j], zr.at[later, far], zss, zrs.at[later, far], at(there, y))

    last = nz - 3

    def straight(j):
        target = at(z, across)
        n = j - (last + 1 - ND)
        return remote(ds.at[n], dr.at[n], dss, drs.at[n], target)

    def neighbour(side):
        there = at((z + (1, -1)[side] + nz) % nz, y)
        return remote(fs.at[side], fr.at[side], fss, frs.at[side], there)

    def zget(slot, far):
        remote(zs.at[0], zr.at[slot, far], zss, zrs.at[slot, far], y_up).wait_recv()
        return get(zr.at[slot, far], 2)

    def project(j, place):
        for copy in load(place):
            copy.wait()
        a = jnp.dot(pin[0], xa[place], preferred_element_type=jnp.float32)
        g = jnp.dot(pout[0], xg[place], preferred_element_type=jnp.float32)
        for d in range(NY):
            pa[j, d] = a[:, d * T : (d + 1) * T]
            pg[j, d] = g[:, d * T : (d + 1) * T]

    def first_hop(j):
        put(h1s.at[j, 0], [pa[j, across], pg[j, up]])
        put(h1s.at[j, 1], [pg[j, across], pa[j, down]])

    def send_first_hop(j):
        hop1(j, 0).start()
        hop1(j, 1).start()

    def send_straight(j):
        put(ds.at[j - (last + 1 - ND)], [pa[j, across], pg[j, across]])
        straight(j).start()
        put(h1s.at[j, 0], [pa[j, up], pg[j, up]])
        hop1(j, 0).start()
        put(h1s.at[j, 1], [pa[j, down], pg[j, down]])
        hop1(j, 1).start()

    def to_neighbour(side):
        place = nz - 3 + side
        project(place, place)
        put(fs.at[side], [p[place, d] for d in range(NY) for p in (pa, pg)])

    def from_neighbour(side):
        neighbour(side).wait_recv()
        pieces = get(fr.at[side], 2 * NY)
        for d in range(NY):
            pa[last, d] += pieces[2 * d]
            pg[last, d] += pieces[2 * d + 1]

    def pass_on(j):
        hop1(j, 0).wait_recv()
        a_on, g_here = get(h1r.at[j, 0], 2)
        put(h2s.at[j, 0], [a_on + pa[j, up]])
        hop2(j, 0).start()
        hop1(j, 1).wait_recv()
        g_on, a_here = get(h1r.at[j, 1], 2)
        put(h2s.at[j, 1], [g_on + pg[j, down]])
        hop2(j, 1).start()
        total[j, 0] = a_here + pa[j, y]
        total[j, 1] = g_here + pg[j, y]

    def finish_y(j):
        hop2(j, 0).wait_recv()
        hop2(j, 1).wait_recv()
        (a,) = get(h2r.at[j, 0], 1)
        (g,) = get(h2r.at[j, 1], 1)
        total[j, 0] += a
        total[j, 1] += g

    def finish_straight(j):
        hop1(j, 0).wait_recv()
        a0, g0 = get(h1r.at[j, 0], 2)
        hop1(j, 1).wait_recv()
        a1, g1 = get(h1r.at[j, 1], 2)
        straight(j).wait_recv()
        a2, g2 = get(dr.at[j - (last + 1 - ND)], 2)
        total[j, 0] = a0 + a1 + a2 + pa[j, y]
        total[j, 1] = g0 + g1 + g2 + pg[j, y]

    def along_z(j):
        @pl.when(j <= last - ND)
        def _():
            finish_y(j)

        @pl.when(j > last - ND)
        def _():
            finish_straight(j)

        h = (nz - j) // 2

        @pl.when((h % 2 == 0) & (j > 0))
        def _():
            a_in, g_in = zget(j, 0)
            total[j, 0] += a_in
            total[j, 1] += g_in

            @pl.when((h < half - 2) | (j % 2 == 1))
            def _():
                a_in, g_in = zget(j, 1)
                total[j, 0] += a_in
                total[j, 1] += g_in

        put(zs.at[j], [total[j, 0], total[j, 1]])
        zstep(j).start()

    lanes = lax.broadcasted_iota(jnp.int32, (tr.shape[0], T), 1) < R

    def widen(j):
        tile = tr[:, pl.ds(pl.multiple_of(j * T, T), T)].astype(jnp.float32)
        turned = pltpu.roll(tile, R, 1)
        first = jnp.concatenate(
            [jnp.where(lanes, tile, 0.0), jnp.where(lanes, turned, 0.0)], axis=1
        )
        second = jnp.concatenate(
            [jnp.where(lanes, 0.0, turned), jnp.where(lanes, 0.0, tile)], axis=1
        )
        wide[j] = jnp.concatenate([first, second], axis=0).astype(jnp.bfloat16)

    def turn(i, _):
        @pl.when(i == 3)
        def _():
            pl.semaphore_wait(told_1, len(tell_1))
            tell(tell_2, told_2)

        @pl.when(i == LAG2)
        def _():
            pl.semaphore_wait(told_2, len(tell_2))

        @pl.when((i > 0) & (i < last))
        def _():
            project(i, i)

        @pl.when((i > 0) & (i <= last - ND))
        def _():
            first_hop(i)
            send_first_hop(i)

        @pl.when((i > last - ND) & (i < last))
        def _():
            send_straight(i)

        @pl.when(i == last)
        def _():
            project(last, nz - 1)
            from_neighbour(0)
            from_neighbour(1)
            send_straight(last)

        @pl.when((i >= LAG1) & (i <= last - ND + LAG1))
        def _():
            pass_on(i - LAG1)

        @pl.when(i >= LAG2)
        def _():
            along_z(i - LAG2)

        @pl.when(i < WIDEN)
        def _():
            for n in range(R // 2 // WIDEN):
                widen(i * (R // 2 // WIDEN) + n)

        return 0

    for copy in small:
        copy.wait()
    project(0, 0)
    first_hop(0)
    to_neighbour(0)
    to_neighbour(1)
    pl.semaphore_wait(barrier, len(greeted))
    send_first_hop(0)
    tell(tell_1, told_1)
    neighbour(0).start()
    neighbour(1).start()
    load_train.wait()
    lax.fori_loop(0, last + LAG2, turn, 0)

    two = jnp.concatenate([pci[0], pci[0]], axis=1)
    two = jnp.concatenate([two, two], axis=0)
    row_low = lax.broadcasted_iota(jnp.int32, (T, T), 0) < R
    lane_low = lax.broadcasted_iota(jnp.int32, (T, T), 1) < R
    pi2[...] = jnp.where(row_low == lane_low, two, 0.0)

    finish_straight(last)
    a, g = total[last, 0], total[last, 1]
    for slot in (nz - 1, nz):
        a_in, g_in = zget(slot, 1)
        a = a + a_in
        g = g + g_in
    a2 = jnp.where(row_low == lane_low, jnp.concatenate([a, a], axis=0), 0.0)
    high = lax.Precision.HIGHEST
    sketch = lax.dot_general(g, a2, NT, precision=high, preferred_element_type=jnp.float32)
    sketch = sketch * (1.0 / 64)
    left = jnp.dot(pco[0], sketch, precision=high, preferred_element_type=jnp.float32)
    both = jnp.dot(left, pi2[...], precision=high, preferred_element_type=jnp.float32)
    own = both.astype(jnp.bfloat16)
    ag[ex] = own

    def spread(e, values):
        xf[pl.ds(e, R, stride=ne), :] = values.astype(jnp.float32)

    def away(t):
        d = (t + 1) // 2
        return (z + jnp.where(t % 2 == 1, -d, d) + nz) % nz

    def gz(t, later, step):
        e = away(t) * NY + y
        return remote(ag.at[e], ag.at[e], azs, azr.at[later], at((z + step + nz) % nz, y))

    def gy1(t, way):
        e = away(t) * NY + y
        return remote(ag.at[e], ag.at[e], y1s, y1r.at[t, way], (y_up, y_down)[way])

    def gy1_wait(t, way):
        e = away(t) * NY + (down, up)[way]
        remote(ag.at[e], ag.at[e], y1s, y1r.at[t, way], (y_up, y_down)[way]).wait_recv()
        return e

    direct = hub + XD
    for d in [hub] + list(range(hub + 1, direct + 1)) + list(range(hub - 1, 0, -1)):
        gz(0, 2 * d - 1, d).start()
        gz(0, 2 * d, -d).start()
    own_across = remote(ag.at[ex], ag.at[ex], y2s, y2r.at[0, 0], at(z, across))
    own_across.start()
    gy1(0, 0).start()
    gy1(0, 1).start()


    for sent, sem in ((h1s, h1ss), (h2s, h2ss), (ds, dss), (fs, fss), (zs, zss)):
        remote(sent, sent, sem, azr.at[0], y_up).wait_send()

    first = 2 * direct + 1

    def chunk(n):
        pair, side = (n - 1) // 2, (n - 1) % 2
        early = 2 * jnp.where(pair < hub, hub - pair, pair + 1) - 1 + side
        m = n - first - 1
        late = jnp.where(n == first, nz - 1, nz - 3 - 2 * (m // 2) + (m + 2) % 2)
        return jnp.where(n == 0, 0, jnp.where(n < first, early, late))

    def arrived(t):
        gz(t, t, 1).wait_recv()

    arrived(2 * hub - 1)
    for d in range(half, direct, -1):
        gz(2 * hub - 1, 2 * d - 1, d - hub).start()
    arrived(2 * hub)
    for d in range(half - 1, direct, -1):
        gz(2 * hub, 2 * d, hub - d).start()

    def forward(n, _):
        t = chunk(n)

        @pl.when(n > 2)
        def _():
            arrived(t)

        gy3(t, y).start()
        gy1(t, 0).start()
        gy1(t, 1).start()
        return 0

    def gy3(t, yy):
        e = away(t) * NY + yy
        return remote(ag.at[e], ag.at[e], y2s, y2r.at[t, 0], at(z, across))

    def forward_late(n, _):
        t = chunk(n)
        arrived(t)
        gy3(t, y).start()
        gy1(t, 0).start()
        gy1(t, 1).start()
        return 0

    def spread_late(n, _):
        t = chunk(n)
        e = away(t) * NY + y
        spread(e, ag[e])
        for way in range(2):
            e = gy1_wait(t, way)
            spread(e, ag[e])
        gy3(t, across).wait_recv()
        e = away(t) * NY + across
        spread(e, ag[e])
        return 0

    lax.fori_loop(1, first, forward, 0)
    lax.fori_loop(first, nz, forward_late, 0)
    lax.fori_loop(0, first, spread_late, 0)
    lax.fori_loop(first, nz, spread_late, 0)

    def score(j, acc):
        x0 = xf[pl.ds(pl.multiple_of(2 * j * ne, 8), ne), :]
        x1 = xf[pl.ds(pl.multiple_of((2 * j + 1) * ne, 8), ne), :]
        x = jnp.concatenate([x0, x1], axis=1).astype(jnp.bfloat16)
        return acc + lax.dot_general(x, wide[j], NT, preferred_element_type=jnp.float32)

    count = wide.shape[1]
    scores = lax.fori_loop(0, R // 2, score, jnp.zeros((ne, count), jnp.float32), unroll=8)
    part[...] = jnp.concatenate([scores, jnp.zeros((ne, T - count), jnp.float32)], axis=1)

    rows = ne // nl

    def layer_copy(step):
        target = (layer + step) % nl
        block = pl.ds(pl.multiple_of(target * rows, 8), rows)
        return remote(part.at[block], lr.at[step - 1], lss, lrs.at[step - 1], (ex, target))

    for step in range(1, nl):
        layer_copy(step).start()
    remote(ag.at[0 : nz - 1], ag.at[0 : nz - 1], azs, azr.at[0], y_up).wait_send()
    remote(ag.at[0 : 2 * nz], ag.at[0 : 2 * nz], y1s, y1r.at[0, 0], y_up).wait_send()
    remote(ag.at[0:nz], ag.at[0:nz], y2s, y2r.at[0, 0], y_up).wait_send()
    result = part[pl.ds(pl.multiple_of(layer * rows, 8), rows), :]
    for step in range(1, nl):
        layer_copy(step).wait_recv()
        result = result + lr[step - 1]
    out[...] = result
    remote(lr, lr, lss, lrs.at[0], y_up).wait_send()


def on_device(nz, nl, query_acts, query_grads, proj_in, proj_out, precond_out, precond_in, train_sketch):
    ff, d = query_acts.shape[1], query_grads.shape[1]
    examples = train_sketch.shape[1]
    ne = nz * NY
    rows = ne // nl
    bf16, f32 = jnp.bfloat16, jnp.float32
    dma = pltpu.SemaphoreType.DMA
    vmem = pl.BlockSpec(memory_space=pltpu.VMEM)
    hbm = pl.BlockSpec(memory_space=pl.ANY)
    summed = pl.pallas_call(
        functools.partial(kernel, nz, nl),
        out_shape=jax.ShapeDtypeStruct((rows, T), f32),
        in_specs=[hbm] * 7,
        out_specs=vmem,
        scratch_shapes=[
            pltpu.VMEM(proj_in.shape, bf16),
            pltpu.VMEM(proj_out.shape, bf16),
            pltpu.VMEM(precond_out.shape, f32),
            pltpu.VMEM(precond_in.shape, f32),
            pltpu.VMEM((nz, ff, NY * T), bf16),
            pltpu.VMEM((nz, d, NY * T), bf16),
            pltpu.VMEM((nz, NY, R, T), f32),
            pltpu.VMEM((nz, NY, R, T), f32),
            pltpu.VMEM((nz, 2, R, T), f32),
            pltpu.VMEM((nz - 2, 2, 2 * R + 16, T), bf16),
            pltpu.VMEM((nz - 2, 2, 2 * R + 16, T), bf16),
            pltpu.VMEM((nz - 2 - ND, 2, R + 16, T), bf16),
            pltpu.VMEM((nz - 2 - ND, 2, R + 16, T), bf16),
            pltpu.VMEM((ND, 2 * R + 16, T), bf16),
            pltpu.VMEM((ND, 2 * R + 16, T), bf16),
            pltpu.VMEM((2, 2 * NY * R + 16, T), bf16),
            pltpu.VMEM((2, 2 * NY * R + 16, T), bf16),
            pltpu.VMEM((nz - 3, 2 * R + 16, T), bf16),
            pltpu.VMEM((nz + 1, 2, 2 * R + 16, T), bf16),
            pltpu.VMEM((ne, R, T), bf16),
            pltpu.VMEM((R * ne, T), f32),
            pltpu.VMEM((examples, R * R), bf16),
            pltpu.VMEM((R // 2, 2 * examples, 2 * T), bf16),
            pltpu.VMEM((T, T), f32),
            pltpu.VMEM((ne, T), f32),
            pltpu.VMEM((nl - 1, rows, T), f32),
            dma((4,)), dma((nz,)), dma((nz,)), dma,
            dma, dma((nz, 2)), dma, dma((nz, 2)), dma, dma((ND,)), dma, dma((2,)),
            dma, dma((nz + 1, 2)), pltpu.SemaphoreType.REGULAR, pltpu.SemaphoreType.REGULAR,
            dma, dma((nz,)), dma, dma((nz, 2)), dma, dma((nz, 2)),
            dma, dma((nl - 1,)),
        ],
        compiler_params=pltpu.CompilerParams(
            collective_id=0, has_side_effects=True, vmem_limit_bytes=60 * 2**20
        ),
    )(query_acts, query_grads, proj_in, proj_out, precond_out, precond_in, train_sketch)
    return summed[:, : 2 * examples].reshape(2 * rows, examples)


def solution(mesh):
    nz, nl = mesh.shape["ex"] // NY, mesh.shape["layer"]
    placed = (
        P("layer", "ex", None),
        P("layer", "ex", None),
        P("layer", None, "ex"),
        P("layer", None, "ex"),
        P("layer", None, None),
        P("layer", None, None),
        P("layer", "ex", None),
    )
    return jax.shard_map(
        functools.partial(on_device, nz, nl),
        mesh=mesh, in_specs=placed, out_specs=P("layer", "ex"), check_vma=False,
    )
```
